512 devices in a mesh: dp: 64 (over z, x), tensor: 8 (over y, core).
Axes of the slice: x: 4, y: 4, z: 16, core: 2. Of those that a mesh axis runs over, the one named last changes fastest.
Arguments:
- grads: bfloat16 [1, 64, 768, 8192], P(None, 'dp', 'tensor'), may hold values from -12 to 12
- error: bfloat16 [1, 64, 768, 8192], P(None, 'dp', 'tensor'), may hold values from -6 to 6
- init_q: bfloat16 [8192, 64], P('tensor'), may hold values from -0.0625 to 0.0625
Outputs:
- new_error: bfloat16 [1, 64, 768, 8192], P(None, 'dp', 'tensor')
- p_factor: float32 [1, 768, 64], P(None, 'tensor')
- q_factor: float32 [8192, 64], P('tensor')
The draws below stay inside these ranges and needn't reach their ends.
All inputs are finite; a program needn't handle non-finite values.
Results may differ from the reference program's by a relative error of at most 0.018.
Values may be sent and summed in bfloat16 or wider, within the bound.
A program may use at most 64 MiB of HBM per device.

```python
import jax
import jax.numpy as jnp
from jax import lax

D = 8192
RANK = 64
LAYERS = 1
ITERS = 2
ROWS_DEV = 96
ROWS = 768
REPLICAS = 64
N_DP = 64
N_TENSOR = 8


def block_levels(key, extent, shards, smallest, top_value):
    def one(axis_at, shards_of):
        heights = jax.random.uniform(jax.random.fold_in(jax.random.fold_in(key, 6), axis_at), (shards_of,), jnp.float32, smallest / len(shards), top_value / len(shards))
        return jnp.repeat(jnp.exp(heights), extent[axis_at] // shards_of).reshape((-1,) + (1,) * (len(extent) - axis_at - 1))

    factor_of = one(*shards[0])
    for cut in shards[1:]:
        factor_of = factor_of * one(*cut)
    return factor_of


def noise(own_key, extent, scale, limit, shards=(), kind=jnp.bfloat16):
    factor_of = block_levels(own_key, extent, shards, -0.22, 0.18) if shards else 1.0
    array = jax.random.normal(own_key, extent, jnp.float32) * scale * factor_of
    return jnp.minimum(jnp.maximum(array, -limit), limit).astype(kind)


def setup_inputs(seed: int = 0) -> dict:
    keys = jax.random.split(jax.random.key(seed), 4)
    return {
        "grads": noise(keys[0], (LAYERS, REPLICAS, ROWS, D), 2.0, 12.0, ((1, 64), (2, 8))),
        "error": noise(keys[1], (LAYERS, REPLICAS, ROWS, D), 1.0, 6.0, ((1, 64), (2, 8))),
        "init_q": noise(keys[2], (D, LAYERS * RANK), D ** -0.5, 0.0625, ((0, 8),)),
    }


shift_value = 0.05

def rounded_sum(grad_one, error_one):
    summed = grad_one.astype(jnp.float32) + error_one.astype(jnp.float32)
    return lax.optimization_barrier(summed.astype(jnp.bfloat16)).astype(jnp.float32)

def reference(grads, error, init_q):
    grads_moved = jnp.moveaxis(grads, 1, 0)
    error_moved = jnp.moveaxis(error, 1, 0)
    q_low = init_q
    p_low = None
    p_hat = None
    q_avg = None
    for iteration in range(ITERS):
        q_three = q_low.astype(jnp.float32).reshape(D, LAYERS, RANK)

        def add_p(accum, pair):
            block = rounded_sum(pair[0], pair[1])
            return (accum + jnp.einsum('lrd,dlk->lrk', block, q_three), None)
        p_total, _ = lax.scan(add_p, jnp.zeros((LAYERS, ROWS, RANK), jnp.float32), (grads_moved, error_moved))
        p_avg = p_total / N_DP
        gram = jnp.einsum('lrk,lrj->lkj', p_avg, p_avg, precision=lax.Precision.HIGHEST)
        gram = gram + shift_value * jnp.eye(RANK, dtype=jnp.float32)
        lower_factor = jnp.linalg.cholesky(gram)
        p_hat = lax.linalg.triangular_solve(lower_factor, p_avg, left_side=False, lower=True, transpose_a=True)
        p_low = p_hat.astype(jnp.bfloat16)
        p_blocks = p_low.astype(jnp.float32).reshape(LAYERS, N_TENSOR, ROWS_DEV, RANK)

        def add_q(accum, pair):
            block = rounded_sum(pair[0], pair[1]).reshape(LAYERS, N_TENSOR, ROWS_DEV, D)
            terms = jnp.einsum('ltrd,ltrk->tdlk', block, p_blocks)
            terms = lax.optimization_barrier(terms.astype(jnp.bfloat16)).astype(jnp.float32)
            return (accum + jnp.sum(terms, axis=0).reshape(D, LAYERS * RANK), None)
        q_total, _ = lax.scan(add_q, jnp.zeros((D, LAYERS * RANK), jnp.float32), (grads_moved, error_moved))
        q_avg = q_total / N_DP
        q_low = q_avg.astype(jnp.bfloat16)
    q_final = q_low.astype(jnp.float32).reshape(D, LAYERS, RANK)
    approx = jnp.einsum('lrk,dlk->lrd', p_low.astype(jnp.float32), q_final)

    def one_error(pair):
        summed = pair[0].astype(jnp.float32) + pair[1].astype(jnp.float32)
        return (summed - approx).astype(jnp.bfloat16)
    new_error = jnp.moveaxis(lax.map(one_error, (grads_moved, error_moved)), 0, 1)
    return (new_error, p_hat, q_avg)
```

```python
import jax
import jax.numpy as jnp
from jax import lax
from jax.experimental import pallas as pl
from jax.experimental.pallas import tpu as pltpu
from jax.sharding import PartitionSpec as P

F32 = jnp.float32
BF16 = jnp.bfloat16
MESH = pl.DeviceIdType.MESH
HIGH = lax.Precision.HIGHEST
NZ, NX, NY, NT = 16, 4, 4, 8
ROWS, COLS, RANK = 96, 8192, 64
SHIFT = 0.05
REPLICAS = 64
NT_DIMS = (((1,), (1,)), ((), ()))


def inverse_factor(gram_wide):
    n, k = RANK, 8
    lane = lax.broadcasted_iota(jnp.int32, (n, 2 * n), 1)
    row = lax.broadcasted_iota(jnp.int32, (n, 2 * n), 0)
    a = gram_wide + jnp.where(lane == row, SHIFT, 0.0) + jnp.where(lane == row + n, 1.0, 0.0)
    for first in range(0, n, k):
        cols = [jnp.broadcast_to(a[:, first + i : first + i + 1], (n, 2 * n)) for i in range(k)]
        rows = [jnp.broadcast_to(a[first + i : first + i + 1, :], (n, 2 * n)) for i in range(k)]
        for i in range(k):
            j = first + i
            f = jnp.where(row > j, cols[i] * (1.0 / cols[i][j : j + 1, :]), 0.0)
            for m in range(i + 1, k):
                cols[m] = cols[m] - f * cols[m][j : j + 1, :]
                rows[m] = rows[m] - f[first + m : first + m + 1, :] * rows[i]
            a = a - f * rows[i]
    pivot = jnp.sum(jnp.where(lane == row, a, 0.0), axis=1, keepdims=True)
    return jnp.where(lane >= n, a, 0.0) * lax.rsqrt(pivot)


def kernel(
    g_hbm, e_hbm, q_hbm, out, pf, qf,
    gv, ev, m2, mz, q0, rr, sz, xrb, mb, part, x_in, px, z1_in, pz, z2_in, pall, phf, phl, q2own, qbuf,
    ld, ring_s, ring_r, q0_s, q0_r, qs_s, qs_r, x_s, x_r, z1_s, z1_r, z2_s, z2_r, xa_s, xa_r, ta_s, ta_r,
    sx_s, sx_r, st_s, st_r, qz_s, qz_r, xy_s, xy_r, sb_s, sb_r,
):
    dp = lax.axis_index("dp")
    t = lax.axis_index("tensor")
    z, x = dp // NX, dp % NX
    y, c = t // 2, t % 2

    def dev(zz, xx, tt):
        return {"dp": zz * NX + xx, "tensor": tt}

    def rcopy(src, dst, s, r, device):
        return pltpu.make_async_remote_copy(src, dst, s, r, device_id=device, device_id_type=MESH)

    barrier = pltpu.get_barrier_semaphore()

    def greet(device):
        pl.semaphore_signal(barrier, inc=1, device_id=device, device_id_type=MESH)

    def greet_z(o, _):
        greet(dev((z + o) % NZ, x, t))
        return 0

    def greet_xy(o, _):
        greet(dev(z, (x + o // NY) % NX, ((y + o % NY) % NY) * 2 + c))
        return 0

    def greet_t(o, _):
        greet(dev(z, x, ((y + o) % NY) * 2 + 1 - c))
        return 0

    lax.fori_loop(1, NZ, greet_z, 0)
    lax.fori_loop(1, NX * NY, greet_xy, 0)
    lax.fori_loop(0, NY, greet_t, 0)

    def load(k, which):
        span = pl.ds(k * 2048, 2048)
        src, dst = ((g_hbm, gv), (e_hbm, ev))[which]
        return pltpu.make_async_copy(src.at[:, span], dst.at[:, span], ld.at[k, which])

    q_load = pltpu.make_async_copy(q_hbm, q0.at[t], ld.at[4, 0])
    q_load.start()
    for k in range(4):
        load(k, 0).start()
        load(k, 1).start()
    mb[:, pl.ds(ROWS, 32), :] = jnp.zeros((NT, 32, 128), BF16)
    part[...] = jnp.zeros((2, 4, 16, 128), F32)
    for k in range(4):
        load(k, 0).wait()
        load(k, 1).wait()

        def add_block(j, _, k=k):
            at = pl.ds(pl.multiple_of(k * 2048 + j * 128, 128), 128)
            block = (gv[:, at].astype(F32) + ev[:, at].astype(F32)).astype(BF16)
            m2[:, at] = block
            mz[k * 16 + j] = block
            return 0

        lax.fori_loop(0, 16, add_block, 0)
    q_load.wait()
    pl.semaphore_wait(barrier, 34)

    def ring(d, s, xb):
        far = 9 - s
        device = dev((z + (1 if d == 0 else NZ - 1)) % NZ, x, t)
        sems = (ring_s.at[d, s - 1, xb], ring_r.at[d, s - 1, xb])
        if s == 1:
            half = pl.ds(48 * d, 48)
            at = ((z + 8) % NZ) * NX + xb
            return rcopy(mz.at[at, half], rr.at[d, 0, xb, half], *sems, device)
        return rcopy(rr.at[d, s - 2, xb], rr.at[d, s - 1, xb], *sems, device)

    def ring_step(s):
        def one(xb, _):
            for d in range(2):
                if s > 1:
                    ring(d, s - 1, xb).wait_recv()
                    far = 9 - s
                    at = ((z + (far if d == 0 else NZ - far)) % NZ) * NX + xb
                    if s == 2:
                        half, rest = pl.ds(48 * d, 48), pl.ds(48 - 48 * d, 48)
                        total = rr[d, 0, xb, half].astype(F32) + mz[at, half].astype(F32)
                        rr[d, 0, xb, half] = total.astype(BF16)
                        rr[d, 0, xb, rest] = mz[at, rest]
                    else:
                        total = rr[d, s - 2, xb].astype(F32) + mz[at].astype(F32)
                        rr[d, s - 2, xb] = total.astype(BF16)
                ring(d, s, xb).start()
            return 0

        lax.fori_loop(0, NX, one, 0)

    def q0_copy(o):
        return rcopy(q0.at[t], q0.at[t], q0_s.at[o - 1], q0_r.at[o - 1], dev(z, x, ((y + o) % NY) * 2 + c))

    def q0_arrived(o):
        slot = q0.at[((y + NY - o) % NY) * 2 + c]
        return rcopy(slot, slot, q0_s.at[o - 1], q0_r.at[o - 1], dev(z, x, ((y + o) % NY) * 2 + c))

    def q0_pass(o, core):
        slot = q0.at[((y + NY - o) % NY) * 2 + core]
        return rcopy(slot, slot, qs_s.at[o], qs_r.at[o], dev(z, x, y * 2 + 1 - c))

    def xcopy(it, o):
        to = (x + o) % NX
        return rcopy(part.at[it, to], x_in.at[it, o - 1], x_s.at[it, o - 1], x_r.at[it, o - 1], dev(z, to, t))

    def z1copy(it, o):
        to = (z // 4) * 4 + (z % 4 + o) % 4
        return rcopy(px.at[it], z1_in.at[it, o - 1], z1_s.at[it, o - 1], z1_r.at[it, o - 1], dev(to, x, t))

    def z2copy(it, o):
        to = (z + 4 * o) % NZ
        return rcopy(pz.at[it], z2_in.at[it, o - 1], z2_s.at[it, o - 1], z2_r.at[it, o - 1], dev(to, x, t))

    def xacopy(it, o, back=0):
        slot = pall.at[it, t, (x + (NX - o) * back) % NX]
        return rcopy(slot, slot, xa_s.at[it, o - 1], xa_r.at[it, o - 1], dev(z, (x + o) % NX, t))

    def tacopy(it, o, back=0):
        slot = pall.at[it, (t + (NT - o) * back) % NT]
        return rcopy(slot, slot, ta_s.at[it, o - 1], ta_r.at[it, o - 1], dev(z, x, (t + o) % NT))

    def start_x(it):
        for o in (2, 1, 3):
            xcopy(it, o).start()

    def x_to_z1(it):
        total = part[it, x]
        for o in (1, 3, 2):
            xcopy(it, o).wait_recv()
            total = total + x_in[it, o - 1]
        px[it] = total
        for o in (2, 1, 3):
            z1copy(it, o).start()

    def z1_to_z2(it):
        total = px[it]
        for o in (1, 3, 2):
            z1copy(it, o).wait_recv()
            total = total + z1_in[it, o - 1]
        pz[it] = total
        for o in (2, 1, 3):
            z2copy(it, o).start()

    def z2_to_xa(it):
        total = pz[it]
        for o in (1, 3, 2):
            z2copy(it, o).wait_recv()
            total = total + z2_in[it, o - 1]
        pall[it, t, x] = total * (1.0 / REPLICAS)
        for o in (2, 1, 3):
            xacopy(it, o).start()

    def xa_to_ta(it):
        for o in (1, 3, 2):
            xacopy(it, o, 1).wait_recv()
        for o in range(1, NT):
            tacopy(it, o).start()

    def finish_p(it):
        for o in range(1, NT):
            tacopy(it, o, 1).wait_recv()
        gram = jnp.zeros((RANK, 128), F32)
        zeros = jnp.zeros((RANK, 128), F32)
        for k in range(NT):
            block = pall[it, k].reshape(RANK, 128)
            wide = jnp.concatenate([block, zeros], axis=0)
            gram = gram + lax.dot_general(block, wide, NT_DIMS, precision=HIGH, preferred_element_type=F32)
        linv = inverse_factor(gram)
        for k in range(NT):
            block = jnp.concatenate([zeros, pall[it, k].reshape(RANK, 128)], axis=0)
            phat = jnp.dot(linv, block, precision=HIGH, preferred_element_type=F32)
            phf[k] = phat
            phl[k] = phat.astype(BF16)

    def next_q():
        total = jnp.zeros((RANK, 128), F32)
        for k in range(NT):
            total = total + jnp.dot(phl[k], mb[k], preferred_element_type=F32)
        return (total * (1.0 / REPLICAS)).astype(BF16)

    def sxcopy(o):
        to = (x + o) % NX
        return rcopy(sz.at[to], xrb.at[o - 1], sx_s.at[o - 1], sx_r.at[o - 1], dev(z, to, t))

    def stcopy(o, back=0):
        slot = mb.at[(t + (NT - o) * back) % NT, pl.ds(0, ROWS)]
        return rcopy(slot, slot, st_s.at[o - 1], st_r.at[o - 1], dev(z, x, (t + o) % NT))

    ring_step(1)
    for o in (2, 1, 3):
        q0_copy(o).start()
    q0_pass(0, c).start()
    ring_step(2)
    ring_step(3)
    for o in (1, 3, 2):
        q0_arrived(o).wait_recv()
        q0_pass(o, c).start()
    ring_step(4)
    for o in range(NY):
        q0_pass(o, 1 - c).wait_recv()
    first_p = jnp.zeros((RANK, ROWS), F32)
    for k in range(NT):
        first_p = first_p + lax.dot_general(q0[k], m2[:, k * 1024 : (k + 1) * 1024], NT_DIMS, preferred_element_type=F32)
    part[0, :, :, 0:ROWS] = first_p.reshape(4, 16, ROWS)
    start_x(0)
    ring_step(5)
    x_to_z1(0)
    ring_step(6)
    z1_to_z2(0)
    ring_step(7)
    ring_step(8)
    z2_to_xa(0)

    def ring_end(xb, _):
        ring(0, 8, xb).wait_recv()
        ring(1, 8, xb).wait_recv()
        total = rr[0, 7, xb].astype(F32) + rr[1, 7, xb].astype(F32) + mz[z * NX + xb].astype(F32)
        sz[xb] = total.astype(BF16)
        return 0

    lax.fori_loop(0, NX, ring_end, 0)
    for o in (2, 1, 3):
        sxcopy(o).start()
    xa_to_ta(0)
    total = sz[x].astype(F32)
    for o in (1, 3, 2):
        sxcopy(o).wait_recv()
        total = total + xrb[o - 1].astype(F32)
    mb[t, pl.ds(0, ROWS)] = total.astype(BF16)
    for o in range(1, NT):
        stcopy(o).start()
    finish_p(0)
    for o in range(1, NT):
        stcopy(o, 1).wait_recv()
    q1 = next_q()
    second_p = lax.dot_general(q1, mb[t], NT_DIMS, preferred_element_type=F32)
    part[1] = second_p.reshape(4, 16, 128)
    start_x(1)
    x_to_z1(1)
    z1_to_z2(1)
    z2_to_xa(1)
    xa_to_ta(1)
    finish_p(1)
    q2own[...] = next_q().reshape(4, 16, 128)

    def qz_slot(k):
        return (NZ - k) * (1 - c) + k * c

    def qz_copy(k):
        to = (z + k * (1 - c) + (NZ - k) * c) % NZ
        return rcopy(q2own.at[y], qbuf.at[y, x, qz_slot(k)], qz_s.at[k - 1], qz_r.at[k - 1], dev(to, x, t))

    @pl.when(c == 0)
    def _():
        qz_copy(8).start()

    for k in range(7, 0, -1):
        qz_copy(k).start()

    @pl.when(c == 1)
    def _():
        qbuf[y, x, 0] = q2own[y]

    own = phf[t]
    pf[...] = own[:, 0:ROWS]
    p_rows = jnp.transpose(own)[0:ROWS, :].astype(BF16)

    for k in range(1, 8):
        qz_copy(k).wait_recv()

    @pl.when(c == 0)
    def _():
        qz_copy(8).wait_recv()

    def xy_copy(o, back=0):
        xo, yo = o // NY, o % NY
        slot = qbuf.at[(y + (NY - yo) * back) % NY, (x + (NX - xo) * back) % NX, pl.ds(8 * (1 - c), 8)]
        to = dev(z, (x + xo) % NX, ((y + yo) % NY) * 2 + c)
        return rcopy(slot, slot, xy_s.at[o - 1], xy_r.at[o - 1], to)

    def sib_copy(o, core):
        xo, yo = o // NY, o % NY
        slot = qbuf.at[(y + NY - yo) % NY, (x + NX - xo) % NX, pl.ds(8 * (1 - core), 8)]
        return rcopy(slot, slot, sb_s.at[o], sb_r.at[o], dev(z, x, y * 2 + 1 - c))

    def xy_start(o, _):
        xy_copy(o).start()
        return 0

    lax.fori_loop(1, NX * NY, xy_start, 0)
    sib_copy(0, c).start()

    def xy_arrive(o, _):
        xy_copy(o, 1).wait_recv()
        sib_copy(o, c).start()
        return 0

    def compute(xo):
        def sib_wait(o, _):
            sib_copy(o, 1 - c).wait_recv()
            return 0

        lax.fori_loop(4 * xo, 4 * xo + 4, sib_wait, 0)
        xx = (x + NX - xo) % NX

        def block(i, _):
            for u in range(4):
                r = 4 * i + u
                at = pl.ds(pl.multiple_of((((z + r) % NZ) * NX + xx) * 128, 128), 128)
                approx = jnp.dot(p_rows, qbuf[:, xx, r].reshape(RANK, 128), preferred_element_type=F32)
                summed = gv[:, at].astype(F32) + ev[:, at].astype(F32)
                out[:, at] = (summed - approx).astype(BF16)
            return 0

        lax.fori_loop(0, 4, block, 0)

    lax.fori_loop(1, 4, xy_arrive, 0)
    for xo in range(1, NX):
        lax.fori_loop(4 * xo, 4 * xo + 4, xy_arrive, 0)
        compute(xo - 1)
    compute(NX - 1)
    for i in range(8):
        r = (2 * t + i // NX + NZ - z) % NZ
        qf[:, i * 128 : (i + 1) * 128] = qbuf[:, i % NX, r].reshape(RANK, 128).astype(F32)

    for s in range(1, 9):
        def ring_sent(xb, _, s=s):
            ring(0, s, xb).wait_send()
            ring(1, s, xb).wait_send()
            return 0

        lax.fori_loop(0, NX, ring_sent, 0)
    for o in range(1, 4):
        q0_copy(o).wait_send()
        sxcopy(o).wait_send()
        for it in range(2):
            xcopy(it, o).wait_send()
            z1copy(it, o).wait_send()
            z2copy(it, o).wait_send()
            xacopy(it, o).wait_send()
    for o in range(NY):
        q0_pass(o, c).wait_send()
    for o in range(1, NT):
        stcopy(o).wait_send()
        qz_copy(o).wait_send()
        tacopy(0, o).wait_send()
        tacopy(1, o).wait_send()

    @pl.when(c == 0)
    def _():
        qz_copy(8).wait_send()

    def xy_sent(o, _):
        xy_copy(o).wait_send()
        return 0

    def sib_sent(o, _):
        sib_copy(o, c).wait_send()
        return 0

    lax.fori_loop(1, NX * NY, xy_sent, 0)
    lax.fori_loop(0, NX * NY, sib_sent, 0)


def body(grads, error, init_q):
    vmem = pl.BlockSpec(memory_space=pltpu.VMEM)
    hbm = pl.BlockSpec(memory_space=pl.ANY)
    dma = pltpu.SemaphoreType.DMA
    scratch = [
        pltpu.VMEM((ROWS, COLS), BF16),
        pltpu.VMEM((ROWS, COLS), BF16),
        pltpu.VMEM((ROWS, COLS), BF16),
        pltpu.VMEM((64, ROWS, 128), BF16),
        pltpu.VMEM((NT, RANK, 1024), BF16),
        pltpu.VMEM((2, 8, NX, ROWS, 128), BF16),
        pltpu.VMEM((NX, ROWS, 128), BF16),
        pltpu.VMEM((3, ROWS, 128), BF16),
        pltpu.VMEM((NT, 128, 128), BF16),
        pltpu.VMEM((2, 4, 16, 128), F32),
        pltpu.VMEM((2, 3, 16, 128), F32),
        pltpu.VMEM((2, 16, 128), F32),
        pltpu.VMEM((2, 3, 16, 128), F32),
        pltpu.VMEM((2, 16, 128), F32),
        pltpu.VMEM((2, 3, 16, 128), F32),
        pltpu.VMEM((2, NT, 4, 16, 128), F32),
        pltpu.VMEM((NT, RANK, 128), F32),
        pltpu.VMEM((NT, RANK, 128), BF16),
        pltpu.VMEM((4, 16, 128), BF16),
        pltpu.VMEM((NY, NX, NZ, 16, 128), BF16),
        dma((5, 2)),
    ]
    for shape in ((2, 8, NX), (3,), (4,), (2, 3), (2, 3), (2, 3), (2, 3), (2, 7), (3,), (7,), (8,), (15,), (16,)):
        scratch += [dma(shape), dma(shape)]
    new_error, p_t, q_t = pl.pallas_call(
        kernel,
        out_shape=(
            jax.ShapeDtypeStruct((ROWS, COLS), BF16),
            jax.ShapeDtypeStruct((RANK, ROWS), F32),
            jax.ShapeDtypeStruct((RANK, 1024), F32),
        ),
        in_specs=[hbm] * 3,
        out_specs=(vmem,) * 3,
        scratch_shapes=scratch,
        compiler_params=pltpu.CompilerParams(collective_id=0, has_side_effects=True, vmem_limit_bytes=48 << 20),
        name="powersgd",
    )(grads[0, 0], error[0, 0], init_q.T)
    return new_error[None, None], p_t.T[None], q_t.T


def solution(mesh):
    in_specs = (P(None, "dp", "tensor", None), P(None, "dp", "tensor", None), P("tensor", None))
    out_specs = (P(None, "dp", "tensor", None), P(None, "tensor", None), P("tensor", None))
    return jax.shard_map(body, mesh=mesh, in_specs=in_specs, out_specs=out_specs, check_vma=False)
```

```python
import jax
import jax.numpy as jnp
from jax import lax
from jax.experimental import pallas as pl
from jax.experimental.pallas import tpu as pltpu
from jax.sharding import PartitionSpec as P

F32 = jnp.float32
BF16 = jnp.bfloat16
MESH = pl.DeviceIdType.MESH
HIGH = lax.Precision.HIGHEST
NZ, NX, NY, NT = 16, 4, 4, 8
ROWS, COLS, RANK = 96, 8192, 64
SHIFT = 0.05
REPLICAS = 64
NT_DIMS = (((1,), (1,)), ((), ()))


def inverse_factor(gram_wide):
    n, k = RANK, 8
    lane = lax.broadcasted_iota(jnp.int32, (n, 2 * n), 1)
    row = lax.broadcasted_iota(jnp.int32, (n, 2 * n), 0)
    a = gram_wide + jnp.where(lane == row, SHIFT, 0.0) + jnp.where(lane == row + n, 1.0, 0.0)
    for first in range(0, n, k):
        cols = [jnp.broadcast_to(a[:, first + i : first + i + 1], (n, 2 * n)) for i in range(k)]
        rows = [jnp.broadcast_to(a[first + i : first + i + 1, :], (n, 2 * n)) for i in range(k)]
        for i in range(k):
            j = first + i
            f = jnp.where(row > j, cols[i] * (1.0 / cols[i][j : j + 1, :]), 0.0)
            for m in range(i + 1, k):
                cols[m] = cols[m] - f * cols[m][j : j + 1, :]
                rows[m] = rows[m] - f[first + m : first + m + 1, :] * rows[i]
            a = a - f * rows[i]
    pivot = jnp.sum(jnp.where(lane == row, a, 0.0), axis=1, keepdims=True)
    return jnp.where(lane >= n, a, 0.0) * lax.rsqrt(pivot)


def kernel(
    g_hbm, e_hbm, q_hbm, out_hbm, pf_hbm, qf_hbm,
    out, pf, qf, gv, ev, m2, mz, q0, rr, sz, xrb, mb, part, x_in, px, z1_in, pz, z2_in, pall, phf, phl, q2own, qbuf,
    ld, ring_s, ring_r, q0_s, q0_r, qs_s, qs_r, x_s, x_r, z1_s, z1_r, z2_s, z2_r, pa_s, pa_r, ps_s, ps_r,
    sx_s, sx_r, st_s, st_r, qz_s, qz_r, xy_s, xy_r, sb_s, sb_r, near, far, st_out,
):
    dp = lax.axis_index("dp")
    t = lax.axis_index("tensor")
    z, x = dp // NX, dp % NX
    y, c = t // 2, t % 2

    def dev(zz, xx, tt):
        return {"dp": zz * NX + xx, "tensor": tt}

    def rcopy(src, dst, s, r, device):
        return pltpu.make_async_remote_copy(src, dst, s, r, device_id=device, device_id_type=MESH)

    sent = []

    def send(make, *args, order):
        for o in order:
            make(*args, o).start()
        sent.append(lambda: [make(*args, o).wait_send() for o in order])

    barrier = pltpu.get_barrier_semaphore()

    def greet(device):
        pl.semaphore_signal(barrier, inc=1, device_id=device, device_id_type=MESH)

    def greet_xy(o, _):
        greet(dev(z, (x + o // NY) % NX, ((y + o % NY) % NY) * 2 + c))
        return 0

    def greet_t(o, _):
        greet(dev(z, x, ((y + o) % NY) * 2 + 1 - c))
        return 0

    for o in (2, NZ - 2, 1, NZ - 1):
        greet(dev((z + o) % NZ, x, t))
    lax.fori_loop(1, NX * NY, greet_xy, 0)
    lax.fori_loop(0, NY, greet_t, 0)

    def greet_far(step, sem):
        for o in (step, NZ - step):
            pl.semaphore_signal(sem, inc=1, device_id=dev((z + o) % NZ, x, t), device_id_type=MESH)

    def load(k, which):
        span = pl.ds(k * 2048, 2048)
        src, dst = ((g_hbm, gv), (e_hbm, ev))[which]
        return pltpu.make_async_copy(src.at[:, span], dst.at[:, span], ld.at[k, which])

    q_load = pltpu.make_async_copy(q_hbm, q0.at[t], ld.at[4, 0])
    q_load.start()
    for k in range(4):
        load(k, 0).start()
        load(k, 1).start()
    mb[:, pl.ds(ROWS, 32), :] = jnp.zeros((NT, 32, 128), BF16)
    part[...] = jnp.zeros((2, 4, 16, 128), F32)
    for k in range(4):
        load(k, 0).wait()
        load(k, 1).wait()

        def add_block(j, _, k=k):
            at = pl.ds(pl.multiple_of(k * 2048 + j * 128, 128), 128)
            block = (gv[:, at].astype(F32) + ev[:, at].astype(F32)).astype(BF16)
            m2[:, at] = block
            mz[k * 16 + j] = block
            return 0

        lax.fori_loop(0, 16, add_block, 0)
    q_load.wait()
    pl.semaphore_wait(barrier, 23)

    def ring(d, s, xb):
        device = dev((z + (1 if d == 0 else NZ - 1)) % NZ, x, t)
        sems = (ring_s.at[d, s - 1, xb], ring_r.at[d, s - 1, xb])
        if s == 1:
            half = pl.ds(48 * d, 48)
            at = ((z + 8) % NZ) * NX + xb
            return rcopy(mz.at[at, half], rr.at[d, 0, xb, half], *sems, device)
        return rcopy(rr.at[d, s - 2, xb], rr.at[d, s - 1, xb], *sems, device)

    def ring_step(s):
        def one(xb, _):
            for d in range(2):
                if s > 1:
                    ring(d, s - 1, xb).wait_recv()
                    hops = 9 - s
                    at = ((z + (hops if d == 0 else NZ - hops)) % NZ) * NX + xb
                    if s == 2:
                        half, rest = pl.ds(48 * d, 48), pl.ds(48 - 48 * d, 48)
                        total = rr[d, 0, xb, half].astype(F32) + mz[at, half].astype(F32)
                        rr[d, 0, xb, half] = total.astype(BF16)
                        rr[d, 0, xb, rest] = mz[at, rest]
                    else:
                        total = rr[d, s - 2, xb].astype(F32) + mz[at].astype(F32)
                        rr[d, s - 2, xb] = total.astype(BF16)
                ring(d, s, xb).start()
            return 0

        lax.fori_loop(0, NX, one, 0)

        def ring_sent(xb, _):
            ring(0, s, xb).wait_send()
            ring(1, s, xb).wait_send()
            return 0

        sent.append(lambda: lax.fori_loop(0, NX, ring_sent, 0))

    def q0_copy(o):
        return rcopy(q0.at[t], q0.at[t], q0_s.at[o - 1], q0_r.at[o - 1], dev(z, x, ((y + o) % NY) * 2 + c))

    def q0_arrived(o):
        slot = q0.at[((y + NY - o) % NY) * 2 + c]
        return rcopy(slot, slot, q0_s.at[o - 1], q0_r.at[o - 1], dev(z, x, ((y + o) % NY) * 2 + c))

    def q0_pass(core, o):
        slot = q0.at[((y + NY - o) % NY) * 2 + core]
        return rcopy(slot, slot, qs_s.at[o], qs_r.at[o], dev(z, x, y * 2 + 1 - c))

    def xcopy(it, o):
        to = (x + o) % NX
        return rcopy(part.at[it, to], x_in.at[it, o - 1], x_s.at[it, o - 1], x_r.at[it, o - 1], dev(z, to, t))

    def z1copy(it, o):
        to = (z // 4) * 4 + (z % 4 + o) % 4
        return rcopy(px.at[it], z1_in.at[it, o - 1], z1_s.at[it, o - 1], z1_r.at[it, o - 1], dev(to, x, t))

    def z2copy(it, o):
        to = (z + 4 * o) % NZ
        return rcopy(pz.at[it], z2_in.at[it, o - 1], z2_s.at[it, o - 1], z2_r.at[it, o - 1], dev(to, x, t))

    def pacopy(it, o, back=0):
        xo, yo = o // NY, o % NY
        slot = pall.at[it, c, (x + (NX - xo) * back) % NX, (y + (NY - yo) * back) % NY]
        to = dev(z, (x + xo) % NX, ((y + yo) % NY) * 2 + c)
        return rcopy(slot, slot, pa_s.at[it, o - 1], pa_r.at[it, o - 1], to)

    def pscopy(it, core, xo):
        slot = pall.at[it, core, (x + NX - xo) % NX]
        return rcopy(slot, slot, ps_s.at[it, xo], ps_r.at[it, xo], dev(z, x, y * 2 + 1 - c))

    def start_x(it):
        send(xcopy, it, order=(2, 1, 3))

    def x_to_z1(it):
        total = part[it, x]
        for o in (1, 3, 2):
            xcopy(it, o).wait_recv()
            total = total + x_in[it, o - 1]
        px[it] = total
        send(z1copy, it, order=(2, 1, 3))

    def z1_to_z2(it):
        total = px[it]
        for o in (1, 3, 2):
            z1copy(it, o).wait_recv()
            total = total + z1_in[it, o - 1]
        pz[it] = total
        send(z2copy, it, order=(2, 1, 3))

    def z2_to_plane(it):
        total = pz[it]
        for o in (1, 3, 2):
            z2copy(it, o).wait_recv()
            total = total + z2_in[it, o - 1]
        pall[it, c, x, y] = total * (1.0 / REPLICAS)

        def start(o, _):
            pacopy(it, o).start()
            return 0

        def leave(o, _):
            pacopy(it, o).wait_send()
            return 0

        lax.fori_loop(1, NX * NY, start, 0)
        sent.append(lambda: lax.fori_loop(1, NX * NY, leave, 0))

    def plane_to_sibling(it):
        def arrive(o, _):
            pacopy(it, o, 1).wait_recv()
            return 0

        for xo in (0, 1, 3, 2):
            lax.fori_loop(max(4 * xo, 1), 4 * xo + 4, arrive, 0)
            send(pscopy, it, c, order=(xo,))

    def finish_p(it):
        for xo in (0, 1, 3, 2):
            pscopy(it, 1 - c, xo).wait_recv()
        gram = jnp.zeros((RANK, 128), F32)
        zeros = jnp.zeros((RANK, 128), F32)
        for k in range(NT):
            block = pall[it, k % 2, :, k // 2].reshape(RANK, 128)
            wide = jnp.concatenate([block, zeros], axis=0)
            gram = gram + lax.dot_general(block, wide, NT_DIMS, precision=HIGH, preferred_element_type=F32)
        linv = inverse_factor(gram)
        for k in range(NT):
            block = jnp.concatenate([zeros, pall[it, k % 2, :, k // 2].reshape(RANK, 128)], axis=0)
            phat = jnp.dot(linv, block, precision=HIGH, preferred_element_type=F32)
            phf[k] = phat
            phl[k] = phat.astype(BF16)

    def next_q():
        total = jnp.zeros((RANK, 128), F32)
        for k in range(NT):
            total = total + jnp.dot(phl[k], mb[k], preferred_element_type=F32)
        return (total * (1.0 / REPLICAS)).astype(BF16)

    def sxcopy(o):
        to = (x + o) % NX
        return rcopy(sz.at[to], xrb.at[o - 1], sx_s.at[o - 1], sx_r.at[o - 1], dev(z, to, t))

    def stcopy(o, back=0):
        slot = mb.at[(t + (NT - o) * back) % NT, pl.ds(0, ROWS)]
        return rcopy(slot, slot, st_s.at[o - 1], st_r.at[o - 1], dev(z, x, (t + o) % NT))

    ring_step(1)
    greet_far(2, near)
    send(q0_copy, order=(2, 1, 3))
    send(q0_pass, c, order=(0,))
    pl.semaphore_wait(near, 2)
    greet_far(4, far)
    ring_step(2)
    ring_step(3)
    for o in (1, 3, 2):
        q0_arrived(o).wait_recv()
        send(q0_pass, c, order=(o,))
    ring_step(4)
    for o in range(NY):
        q0_pass(1 - c, o).wait_recv()
    first_p = jnp.zeros((RANK, ROWS), F32)
    for k in range(NT):
        first_p = first_p + lax.dot_general(q0[k], m2[:, k * 1024 : (k + 1) * 1024], NT_DIMS, preferred_element_type=F32)
    part[0, :, :, 0:ROWS] = first_p.reshape(4, 16, ROWS)
    pl.semaphore_wait(far, 2)
    start_x(0)
    ring_step(5)
    x_to_z1(0)
    ring_step(6)
    z1_to_z2(0)
    ring_step(7)
    ring_step(8)
    z2_to_plane(0)

    def ring_end(xb, _):
        ring(0, 8, xb).wait_recv()
        ring(1, 8, xb).wait_recv()
        total = rr[0, 7, xb].astype(F32) + rr[1, 7, xb].astype(F32) + mz[z * NX + xb].astype(F32)
        sz[xb] = total.astype(BF16)
        return 0

    lax.fori_loop(0, NX, ring_end, 0)
    send(sxcopy, order=(2, 1, 3))
    plane_to_sibling(0)
    total = sz[x].astype(F32)
    for o in (1, 3, 2):
        sxcopy(o).wait_recv()
        total = total + xrb[o - 1].astype(F32)
    mb[t, pl.ds(0, ROWS)] = total.astype(BF16)
    send(stcopy, order=range(1, NT))
    finish_p(0)
    for o in range(1, NT):
        stcopy(o, 1).wait_recv()
    q1 = next_q()
    second_p = lax.dot_general(q1, mb[t], NT_DIMS, preferred_element_type=F32)
    part[1] = second_p.reshape(4, 16, 128)
    start_x(1)
    x_to_z1(1)
    z1_to_z2(1)
    z2_to_plane(1)
    plane_to_sibling(1)
    finish_p(1)
    q2own[...] = next_q().reshape(4, 16, 128)

    def qz_slot(k):
        return (NZ - k) * (1 - c) + k * c

    def qz_copy(k):
        to = (z + k * (1 - c) + (NZ - k) * c) % NZ
        return rcopy(q2own.at[y], qbuf.at[y, x, qz_slot(k)], qz_s.at[k - 1], qz_r.at[k - 1], dev(to, x, t))

    @pl.when(c == 0)
    def _():
        qz_copy(8).start()

    def far_sent():
        @pl.when(c == 0)
        def _():
            qz_copy(8).wait_send()

    sent.append(far_sent)
    send(qz_copy, order=range(7, 0, -1))

    @pl.when(c == 1)
    def _():
        qbuf[y, x, 0] = q2own[y]

    own = phf[t]
    pf[...] = own[:, 0:ROWS]
    pf_copy = pltpu.make_async_copy(pf, pf_hbm, st_out.at[4])
    pf_copy.start()
    p_rows = jnp.transpose(own)[0:ROWS, :].astype(BF16)

    for k in range(1, 8):
        qz_copy(k).wait_recv()

    @pl.when(c == 0)
    def _():
        qz_copy(8).wait_recv()

    def xy_copy(o, back=0):
        xo, yo = o // NY, o % NY
        slot = qbuf.at[(y + (NY - yo) * back) % NY, (x + (NX - xo) * back) % NX, pl.ds(8 * (1 - c), 8)]
        to = dev(z, (x + xo) % NX, ((y + yo) % NY) * 2 + c)
        return rcopy(slot, slot, xy_s.at[o - 1], xy_r.at[o - 1], to)

    def sib_copy(o, core):
        xo, yo = o // NY, o % NY
        slot = qbuf.at[(y + NY - yo) % NY, (x + NX - xo) % NX, pl.ds(8 * (1 - core), 8)]
        return rcopy(slot, slot, sb_s.at[o], sb_r.at[o], dev(z, x, y * 2 + 1 - c))

    def xy_start(o, _):
        xy_copy(o).start()
        return 0

    def xy_sent(o, _):
        xy_copy(o).wait_send()
        return 0

    def sib_sent(o, _):
        sib_copy(o, c).wait_send()
        return 0

    lax.fori_loop(1, NX * NY, xy_start, 0)
    sib_copy(0, c).start()
    sent.append(lambda: lax.fori_loop(1, NX * NY, xy_sent, 0))
    sent.append(lambda: lax.fori_loop(0, NX * NY, sib_sent, 0))

    def xy_arrive(o, _):
        xy_copy(o, 1).wait_recv()
        sib_copy(o, c).start()
        return 0

    def compute(xo):
        def sib_wait(o, _):
            sib_copy(o, 1 - c).wait_recv()
            return 0

        lax.fori_loop(4 * xo, 4 * xo + 4, sib_wait, 0)
        xx = (x + NX - xo) % NX

        def block(i, _):
            for u in range(4):
                r = 4 * i + u
                at = pl.ds(pl.multiple_of((((z + r) % NZ) * NX + xx) * 128, 128), 128)
                approx = jnp.dot(p_rows, qbuf[:, xx, r].reshape(RANK, 128), preferred_element_type=F32)
                summed = gv[:, at].astype(F32) + ev[:, at].astype(F32)
                out[:, at] = (summed - approx).astype(BF16)
                pltpu.make_async_copy(out.at[:, at], out_hbm.at[:, at], st_out.at[xo]).start()
            return 0

        lax.fori_loop(0, 4, block, 0)

    lax.fori_loop(1, 4, xy_arrive, 0)
    for xo in range(1, NX):
        lax.fori_loop(4 * xo, 4 * xo + 4, xy_arrive, 0)
        compute(xo - 1)
    compute(NX - 1)
    for i in range(8):
        r = (2 * t + i // NX + NZ - z) % NZ
        qf[:, i * 128 : (i + 1) * 128] = qbuf[:, i % NX, r].reshape(RANK, 128).astype(F32)

    qf_copy = pltpu.make_async_copy(qf, qf_hbm, st_out.at[5])
    qf_copy.start()
    for wait in sent:
        wait()
    pf_copy.wait()
    qf_copy.wait()
    for xo in range(NX):
        part_of = pl.ds(xo * 2048, 2048)
        pltpu.make_async_copy(out.at[:, part_of], out_hbm.at[:, part_of], st_out.at[xo]).wait()


def emit(a, b, d, out_a, out_b, out_d, va, vb, vd, sem):
    rows = [pl.ds(i * 32, 32) for i in range(3)]
    pieces = [(a.at[r], va.at[r], out_a.at[r]) for r in rows] + [(b, vb, out_b), (d, vd, out_d)]
    loads = [pltpu.make_async_copy(src, mid, sem.at[0, i]) for i, (src, mid, _) in enumerate(pieces)]
    stores = [pltpu.make_async_copy(mid, dst, sem.at[1, i]) for i, (_, mid, dst) in enumerate(pieces)]
    for load in loads:
        load.start()
    for load, store in zip(loads, stores):
        load.wait()
        store.start()
    for store in stores:
        store.wait()


def body(grads, error, init_q):
    hbm = pl.BlockSpec(memory_space=pltpu.HBM)
    dma = pltpu.SemaphoreType.DMA
    scratch = [
        pltpu.VMEM((ROWS, COLS), BF16),
        pltpu.VMEM((RANK, ROWS), F32),
        pltpu.VMEM((RANK, 1024), F32),
        pltpu.VMEM((ROWS, COLS), BF16),
        pltpu.VMEM((ROWS, COLS), BF16),
        pltpu.VMEM((ROWS, COLS), BF16),
        pltpu.VMEM((64, ROWS, 128), BF16),
        pltpu.VMEM((NT, RANK, 1024), BF16),
        pltpu.VMEM((2, 8, NX, ROWS, 128), BF16),
        pltpu.VMEM((NX, ROWS, 128), BF16),
        pltpu.VMEM((3, ROWS, 128), BF16),
        pltpu.VMEM((NT, 128, 128), BF16),
        pltpu.VMEM((2, 4, 16, 128), F32),
        pltpu.VMEM((2, 3, 16, 128), F32),
        pltpu.VMEM((2, 16, 128), F32),
        pltpu.VMEM((2, 3, 16, 128), F32),
        pltpu.VMEM((2, 16, 128), F32),
        pltpu.VMEM((2, 3, 16, 128), F32),
        pltpu.VMEM((2, 2, NX, NY, 16, 128), F32),
        pltpu.VMEM((NT, RANK, 128), F32),
        pltpu.VMEM((NT, RANK, 128), BF16),
        pltpu.VMEM((4, 16, 128), BF16),
        pltpu.VMEM((NY, NX, NZ, 16, 128), BF16),
        dma((5, 2)),
    ]
    for shape in ((2, 8, NX), (3,), (4,), (2, 3), (2, 3), (2, 3), (2, 15), (2, 4), (3,), (7,), (8,), (15,), (16,)):
        scratch += [dma(shape), dma(shape)]
    scratch += [pltpu.SemaphoreType.REGULAR] * 2 + [dma((6,))]
    out_shape = (
        jax.ShapeDtypeStruct((ROWS, COLS), BF16),
        jax.ShapeDtypeStruct((RANK, ROWS), F32),
        jax.ShapeDtypeStruct((RANK, 1024), F32),
    )
    results = pl.pallas_call(
        kernel,
        out_shape=out_shape,
        in_specs=[hbm] * 3,
        out_specs=(hbm,) * 3,
        scratch_shapes=scratch,
        compiler_params=pltpu.CompilerParams(collective_id=0, has_side_effects=True, vmem_limit_bytes=60 << 20),
        name="powersgd",
    )(grads[0, 0], error[0, 0], init_q.T)
    new_error, p_t, q_t = pl.pallas_call(
        emit,
        out_shape=out_shape,
        in_specs=[hbm] * 3,
        out_specs=(hbm,) * 3,
        scratch_shapes=[pltpu.VMEM(o.shape, o.dtype) for o in out_shape] + [dma((2, 5))],
        compiler_params=pltpu.CompilerParams(vmem_limit_bytes=60 << 20),
        name="emit",
    )(*results)
    return new_error[None, None], p_t.T[None], q_t.T


def solution(mesh):
    in_specs = (P(None, "dp", "tensor", None), P(None, "dp", "tensor", None), P("tensor", None))
    out_specs = (P(None, "dp", "tensor", None), P(None, "tensor", None), P("tensor", None))
    return jax.shard_map(body, mesh=mesh, in_specs=in_specs, out_specs=out_specs, check_vma=False)
```

```python
import jax
import jax.numpy as jnp
from jax import lax
from jax.experimental import pallas as pl
from jax.experimental.pallas import tpu as pltpu
from jax.sharding import PartitionSpec as P

F32 = jnp.float32
BF16 = jnp.bfloat16
MESH = pl.DeviceIdType.MESH
HIGH = lax.Precision.HIGHEST
NZ, NX, NY, NT = 16, 4, 4, 8
ROWS, COLS, RANK = 96, 8192, 64
SHIFT = 0.05
REPLICAS = 64
NT_DIMS = (((1,), (1,)), ((), ()))


def inverse_factor(gram_wide):
    n, k = RANK, 8
    lane = lax.broadcasted_iota(jnp.int32, (n, 2 * n), 1)
    row = lax.broadcasted_iota(jnp.int32, (n, 2 * n), 0)
    a = gram_wide + jnp.where(lane == row, SHIFT, 0.0) + jnp.where(lane == row + n, 1.0, 0.0)
    for first in range(0, n, k):
        cols = [jnp.broadcast_to(a[:, first + i : first + i + 1], (n, 2 * n)) for i in range(k)]
        rows = [jnp.broadcast_to(a[first + i : first + i + 1, :], (n, 2 * n)) for i in range(k)]
        for i in range(k):
            j = first + i
            f = jnp.where(row > j, cols[i] * (1.0 / cols[i][j : j + 1, :]), 0.0)
            for m in range(i + 1, k):
                cols[m] = cols[m] - f * cols[m][j : j + 1, :]
                rows[m] = rows[m] - f[first + m : first + m + 1, :] * rows[i]
            a = a - f * rows[i]
    pivot = jnp.sum(jnp.where(lane == row, a, 0.0), axis=1, keepdims=True)
    return jnp.where(lane >= n, a, 0.0) * lax.rsqrt(pivot)


def kernel(
    g_hbm, e_hbm, q_hbm, out_hbm, pf_hbm, qf_hbm,
    out, pf, qf, gv, ev, m2, mz, q0, rr, sz, xrb, mb, part, x_in, px, z1_in, pz, z2_in, pall, phf, phl, q2own, qbuf,
    ld, ring_s, ring_r, q0_s, q0_r, qs_s, qs_r, x_s, x_r, z1_s, z1_r, z2_s, z2_r, pa_s, pa_r, ps_s, ps_r,
    sx_s, sx_r, st_s, st_r, qz_s, qz_r, xy_s, xy_r, sb_s, sb_r, near, far, st_out,
):
    dp = lax.axis_index("dp")
    t = lax.axis_index("tensor")
    z, x = dp // NX, dp % NX
    y, c = t // 2, t % 2

    def dev(zz, xx, tt):
        return {"dp": zz * NX + xx, "tensor": tt}

    def rcopy(src, dst, s, r, device):
        return pltpu.make_async_remote_copy(src, dst, s, r, device_id=device, device_id_type=MESH)

    sent = []

    def send(make, *args, order):
        for o in order:
            make(*args, o).start()
        sent.append(lambda: [make(*args, o).wait_send() for o in order])

    barrier = pltpu.get_barrier_semaphore()

    def greet(device):
        pl.semaphore_signal(barrier, inc=1, device_id=device, device_id_type=MESH)

    def greet_xy(o, _):
        greet(dev(z, (x + o // NY) % NX, ((y + o % NY) % NY) * 2 + c))
        return 0

    def greet_t(o, _):
        greet(dev(z, x, ((y + o) % NY) * 2 + 1 - c))
        return 0

    for o in (2, NZ - 2, 1, NZ - 1):
        greet(dev((z + o) % NZ, x, t))
    lax.fori_loop(1, NX * NY, greet_xy, 0)
    lax.fori_loop(0, NY, greet_t, 0)

    def greet_far(step, sem):
        for o in (step, NZ - step):
            pl.semaphore_signal(sem, inc=1, device_id=dev((z + o) % NZ, x, t), device_id_type=MESH)

    def load(k, which):
        span = pl.ds(k * 2048, 2048)
        src, dst = ((g_hbm, gv), (e_hbm, ev))[which]
        return pltpu.make_async_copy(src.at[:, span], dst.at[:, span], ld.at[k, which])

    q_load = pltpu.make_async_copy(q_hbm, q0.at[t], ld.at[4, 0])
    q_load.start()
    for k in range(4):
        load(k, 0).start()
        load(k, 1).start()
    mb[:, pl.ds(ROWS, 32), :] = jnp.zeros((NT, 32, 128), BF16)
    part[...] = jnp.zeros((2, 4, 16, 128), F32)
    for k in range(4):
        load(k, 0).wait()
        load(k, 1).wait()

        def add_block(j, _, k=k):
            at = pl.ds(pl.multiple_of(k * 2048 + j * 128, 128), 128)
            block = (gv[:, at].astype(F32) + ev[:, at].astype(F32)).astype(BF16)
            m2[:, at] = block
            mz[k * 16 + j] = block
            return 0

        lax.fori_loop(0, 16, add_block, 0)
    q_load.wait()
    pl.semaphore_wait(barrier, 23)

    def ring(d, s, xb):
        device = dev((z + (1 if d == 0 else NZ - 1)) % NZ, x, t)
        sems = (ring_s.at[d, s - 1, xb], ring_r.at[d, s - 1, xb])
        if s == 1:
            half = pl.ds(48 * d, 48)
            at = ((z + 8) % NZ) * NX + xb
            return rcopy(mz.at[at, half], rr.at[d, 0, xb, half], *sems, device)
        return rcopy(rr.at[d, s - 2, xb], rr.at[d, s - 1, xb], *sems, device)

    def ring_step(s):
        def one(xb, _):
            for d in range(2):
                if s > 1:
                    ring(d, s - 1, xb).wait_recv()
                    hops = 9 - s
                    at = ((z + (hops if d == 0 else NZ - hops)) % NZ) * NX + xb
                    if s == 2:
                        half, rest = pl.ds(48 * d, 48), pl.ds(48 - 48 * d, 48)
                        total = rr[d, 0, xb, half].astype(F32) + mz[at, half].astype(F32)
                        rr[d, 0, xb, half] = total.astype(BF16)
                        rr[d, 0, xb, rest] = mz[at, rest]
                    else:
                        total = rr[d, s - 2, xb].astype(F32) + mz[at].astype(F32)
                        rr[d, s - 2, xb] = total.astype(BF16)
                ring(d, s, xb).start()
            return 0

        lax.fori_loop(0, NX, one, 0)

        def ring_sent(xb, _):
            ring(0, s, xb).wait_send()
            ring(1, s, xb).wait_send()
            return 0

        sent.append(lambda: lax.fori_loop(0, NX, ring_sent, 0))

    def q0_copy(o):
        return rcopy(q0.at[t], q0.at[t], q0_s.at[o - 1], q0_r.at[o - 1], dev(z, x, ((y + o) % NY) * 2 + c))

    def q0_arrived(o):
        slot = q0.at[((y + NY - o) % NY) * 2 + c]
        return rcopy(slot, slot, q0_s.at[o - 1], q0_r.at[o - 1], dev(z, x, ((y + o) % NY) * 2 + c))

    def q0_pass(core, o):
        slot = q0.at[((y + NY - o) % NY) * 2 + core]
        return rcopy(slot, slot, qs_s.at[o], qs_r.at[o], dev(z, x, y * 2 + 1 - c))

    def xcopy(it, o):
        to = (x + o) % NX
        return rcopy(part.at[it, to], x_in.at[it, o - 1], x_s.at[it, o - 1], x_r.at[it, o - 1], dev(z, to, t))

    def z1copy(it, i):
        to = (z + (8, 2, 14, 1, 15)[i]) % NZ
        return rcopy(px.at[it], z1_in.at[it, i], z1_s.at[it, i], z1_r.at[it, i], dev(to, x, t))

    def z2copy(it, i):
        to = (z + (5, 11)[i]) % NZ
        return rcopy(pz.at[it], z2_in.at[it, i], z2_s.at[it, i], z2_r.at[it, i], dev(to, x, t))

    def pacopy(it, o, back=0):
        xo, yo = o // NY, o % NY
        slot = pall.at[it, c, (x + (NX - xo) * back) % NX, (y + (NY - yo) * back) % NY]
        to = dev(z, (x + xo) % NX, ((y + yo) % NY) * 2 + c)
        return rcopy(slot, slot, pa_s.at[it, o - 1], pa_r.at[it, o - 1], to)

    def pscopy(it, core, xo):
        slot = pall.at[it, core, (x + NX - xo) % NX]
        return rcopy(slot, slot, ps_s.at[it, xo], ps_r.at[it, xo], dev(z, x, y * 2 + 1 - c))

    def start_x(it):
        send(xcopy, it, order=(2, 1, 3))

    def x_to_z1(it):
        total = part[it, x]
        for o in (1, 3, 2):
            xcopy(it, o).wait_recv()
            total = total + x_in[it, o - 1]
        px[it] = total
        send(z1copy, it, order=range(5))

    def z1_to_z2(it):
        total = px[it]
        for i in (3, 4, 1, 2):
            z1copy(it, i).wait_recv()
            total = total + z1_in[it, i]
        pz[it] = total
        send(z2copy, it, order=range(2))

    def z2_to_plane(it):
        total = pz[it]
        z1copy(it, 0).wait_recv()
        total = total + z1_in[it, 0]
        for i in range(2):
            z2copy(it, i).wait_recv()
            total = total + z2_in[it, i]
        pall[it, c, x, y] = total * (1.0 / REPLICAS)

        def start(o, _):
            pacopy(it, o).start()
            return 0

        def leave(o, _):
            pacopy(it, o).wait_send()
            return 0

        lax.fori_loop(1, NX * NY, start, 0)
        sent.append(lambda: lax.fori_loop(1, NX * NY, leave, 0))

    def plane_to_sibling(it):
        def arrive(o, _):
            pacopy(it, o, 1).wait_recv()
            return 0

        for xo in (0, 1, 3, 2):
            lax.fori_loop(max(4 * xo, 1), 4 * xo + 4, arrive, 0)
            send(pscopy, it, c, order=(xo,))

    def finish_p(it):
        for xo in (0, 1, 3, 2):
            pscopy(it, 1 - c, xo).wait_recv()
        gram = jnp.zeros((RANK, 128), F32)
        zeros = jnp.zeros((RANK, 128), F32)
        for k in range(NT):
            block = pall[it, k % 2, :, k // 2].reshape(RANK, 128)
            wide = jnp.concatenate([block, zeros], axis=0)
            gram = gram + lax.dot_general(block, wide, NT_DIMS, precision=HIGH, preferred_element_type=F32)
        linv = inverse_factor(gram)
        for k in range(NT):
            block = jnp.concatenate([zeros, pall[it, k % 2, :, k // 2].reshape(RANK, 128)], axis=0)
            phat = jnp.dot(linv, block, precision=HIGH, preferred_element_type=F32)
            phf[k] = phat
            phl[k] = phat.astype(BF16)

    def next_q():
        total = jnp.zeros((RANK, 128), F32)
        for k in range(NT):
            total = total + jnp.dot(phl[k], mb[k], preferred_element_type=F32)
        return (total * (1.0 / REPLICAS)).astype(BF16)

    def sxcopy(o):
        to = (x + o) % NX
        return rcopy(sz.at[to], xrb.at[o - 1], sx_s.at[o - 1], sx_r.at[o - 1], dev(z, to, t))

    def stcopy(o, back=0):
        slot = mb.at[(t + (NT - o) * back) % NT, pl.ds(0, ROWS)]
        return rcopy(slot, slot, st_s.at[o - 1], st_r.at[o - 1], dev(z, x, (t + o) % NT))

    ring_step(1)
    greet_far(2, near)
    send(q0_copy, order=(2, 1, 3))
    send(q0_pass, c, order=(0,))
    pl.semaphore_wait(near, 2)
    greet_far(4, far)
    ring_step(2)
    ring_step(3)
    for o in (1, 3, 2):
        q0_arrived(o).wait_recv()
        send(q0_pass, c, order=(o,))
    ring_step(4)
    for o in range(NY):
        q0_pass(1 - c, o).wait_recv()
    first_p = jnp.zeros((RANK, ROWS), F32)
    for k in range(NT):
        first_p = first_p + lax.dot_general(q0[k], m2[:, k * 1024 : (k + 1) * 1024], NT_DIMS, preferred_element_type=F32)
    part[0, :, :, 0:ROWS] = first_p.reshape(4, 16, ROWS)
    pl.semaphore_wait(far, 2)
    start_x(0)
    ring_step(5)
    x_to_z1(0)
    ring_step(6)
    z1_to_z2(0)
    ring_step(7)
    ring_step(8)
    z2_to_plane(0)

    def ring_end(xb, _):
        ring(0, 8, xb).wait_recv()
        ring(1, 8, xb).wait_recv()
        total = rr[0, 7, xb].astype(F32) + rr[1, 7, xb].astype(F32) + mz[z * NX + xb].astype(F32)
        sz[xb] = total.astype(BF16)
        return 0

    lax.fori_loop(0, NX, ring_end, 0)
    send(sxcopy, order=(2, 1, 3))
    plane_to_sibling(0)
    total = sz[x].astype(F32)
    for o in (1, 3, 2):
        sxcopy(o).wait_recv()
        total = total + xrb[o - 1].astype(F32)
    mb[t, pl.ds(0, ROWS)] = total.astype(BF16)
    send(stcopy, order=range(1, NT))
    finish_p(0)
    for o in range(1, NT):
        stcopy(o, 1).wait_recv()
    q1 = next_q()
    second_p = lax.dot_general(q1, mb[t], NT_DIMS, preferred_element_type=F32)
    part[1] = second_p.reshape(4, 16, 128)
    start_x(1)
    x_to_z1(1)
    z1_to_z2(1)
    z2_to_plane(1)
    plane_to_sibling(1)
    finish_p(1)
    q2own[...] = next_q().reshape(4, 16, 128)

    def qz_slot(k):
        return (NZ - k) * (1 - c) + k * c

    def qz_copy(k):
        to = (z + k * (1 - c) + (NZ - k) * c) % NZ
        return rcopy(q2own.at[y], qbuf.at[y, x, qz_slot(k)], qz_s.at[k - 1], qz_r.at[k - 1], dev(to, x, t))

    @pl.when(c == 0)
    def _():
        qz_copy(8).start()

    def far_sent():
        @pl.when(c == 0)
        def _():
            qz_copy(8).wait_send()

    sent.append(far_sent)
    send(qz_copy, order=range(7, 0, -1))

    @pl.when(c == 1)
    def _():
        qbuf[y, x, 0] = q2own[y]

    own = phf[t]
    pf[...] = own[:, 0:ROWS]
    pf_copy = pltpu.make_async_copy(pf, pf_hbm, st_out.at[4])
    pf_copy.start()
    p_rows = jnp.transpose(own)[0:ROWS, :].astype(BF16)

    def plane_span(half, core):
        return pl.ds((12 - 4 * half) * (1 - core) + 4 * half * core, 4)

    def xy_copy(half, o, back=0):
        xo, yo = o // NY, o % NY
        slot = qbuf.at[(y + (NY - yo) * back) % NY, (x + (NX - xo) * back) % NX, plane_span(half, c)]
        to = dev(z, (x + xo) % NX, ((y + yo) % NY) * 2 + c)
        return rcopy(slot, slot, xy_s.at[half, o - 1], xy_r.at[half, o - 1], to)

    def sib_copy(half, o, core):
        xo, yo = o // NY, o % NY
        slot = qbuf.at[(y + NY - yo) % NY, (x + NX - xo) % NX, plane_span(half, core)]
        return rcopy(slot, slot, sb_s.at[half, o], sb_r.at[half, o], dev(z, x, y * 2 + 1 - c))

    def to_plane(half):
        def start(o, _):
            xy_copy(half, o).start()
            return 0

        def leave(o, _):
            xy_copy(half, o).wait_send()
            return 0

        def leave_sibling(o, _):
            sib_copy(half, o, c).wait_send()
            return 0

        lax.fori_loop(1, NX * NY, start, 0)
        sib_copy(half, 0, c).start()
        sent.append(lambda: lax.fori_loop(1, NX * NY, leave, 0))
        sent.append(lambda: lax.fori_loop(0, NX * NY, leave_sibling, 0))

    def from_plane(half, xo):
        def arrive(o, _):
            xy_copy(half, o, 1).wait_recv()
            sib_copy(half, o, c).start()
            return 0

        lax.fori_loop(max(4 * xo, 1), 4 * xo + 4, arrive, 0)

    def compute(half, xo):
        def sib_wait(o, _):
            sib_copy(half, o, 1 - c).wait_recv()
            return 0

        lax.fori_loop(4 * xo, 4 * xo + 4, sib_wait, 0)
        xx = (x + NX - xo) % NX
        for first in (12 - 4 * half, 4 * half):
            for r in range(first, first + 4):
                at = pl.ds(pl.multiple_of((((z + r) % NZ) * NX + xx) * 128, 128), 128)
                approx = jnp.dot(p_rows, qbuf[:, xx, r].reshape(RANK, 128), preferred_element_type=F32)
                summed = gv[:, at].astype(F32) + ev[:, at].astype(F32)
                out[:, at] = (summed - approx).astype(BF16)
                pltpu.make_async_copy(out.at[:, at], out_hbm.at[:, at], st_out.at[xo]).start()

    for k in range(1, 4):
        qz_copy(k).wait_recv()

    @pl.when(c == 0)
    def _():
        qz_copy(4).wait_recv()

    to_plane(0)

    @pl.when(c == 1)
    def _():
        qz_copy(4).wait_recv()

    for k in range(5, 8):
        qz_copy(k).wait_recv()

    @pl.when(c == 0)
    def _():
        qz_copy(8).wait_recv()

    to_plane(1)
    for xo in range(NX):
        from_plane(0, xo)
    for xo in range(NX):
        compute(0, xo)
        from_plane(1, xo)
    for xo in range(NX):
        compute(1, xo)
    for i in range(8):
        r = (2 * t + i // NX + NZ - z) % NZ
        qf[:, i * 128 : (i + 1) * 128] = qbuf[:, i % NX, r].reshape(RANK, 128).astype(F32)

    qf_copy = pltpu.make_async_copy(qf, qf_hbm, st_out.at[5])
    qf_copy.start()
    for wait in sent:
        wait()
    pf_copy.wait()
    qf_copy.wait()
    for xo in range(NX):
        part_of = pl.ds(xo * 2048, 2048)
        pltpu.make_async_copy(out.at[:, part_of], out_hbm.at[:, part_of], st_out.at[xo]).wait()


def emit(a, b, d, out_a, out_b, out_d, va, vb, vd, sem):
    rows = [pl.ds(i * 32, 32) for i in range(3)]
    pieces = [(a.at[r], va.at[r], out_a.at[r]) for r in rows] + [(b, vb, out_b), (d, vd, out_d)]
    loads = [pltpu.make_async_copy(src, mid, sem.at[0, i]) for i, (src, mid, _) in enumerate(pieces)]
    stores = [pltpu.make_async_copy(mid, dst, sem.at[1, i]) for i, (_, mid, dst) in enumerate(pieces)]
    for load in loads:
        load.start()
    for load, store in zip(loads, stores):
        load.wait()
        store.start()
    for store in stores:
        store.wait()


def body(grads, error, init_q):
    hbm = pl.BlockSpec(memory_space=pltpu.HBM)
    dma = pltpu.SemaphoreType.DMA
    scratch = [
        pltpu.VMEM((ROWS, COLS), BF16),
        pltpu.VMEM((RANK, ROWS), F32),
        pltpu.VMEM((RANK, 1024), F32),
        pltpu.VMEM((ROWS, COLS), BF16),
        pltpu.VMEM((ROWS, COLS), BF16),
        pltpu.VMEM((ROWS, COLS), BF16),
        pltpu.VMEM((64, ROWS, 128), BF16),
        pltpu.VMEM((NT, RANK, 1024), BF16),
        pltpu.VMEM((2, 8, NX, ROWS, 128), BF16),
        pltpu.VMEM((NX, ROWS, 128), BF16),
        pltpu.VMEM((3, ROWS, 128), BF16),
        pltpu.VMEM((NT, 128, 128), BF16),
        pltpu.VMEM((2, 4, 16, 128), F32),
        pltpu.VMEM((2, 3, 16, 128), F32),
        pltpu.VMEM((2, 16, 128), F32),
        pltpu.VMEM((2, 5, 16, 128), F32),
        pltpu.VMEM((2, 16, 128), F32),
        pltpu.VMEM((2, 2, 16, 128), F32),
        pltpu.VMEM((2, 2, NX, NY, 16, 128), F32),
        pltpu.VMEM((NT, RANK, 128), F32),
        pltpu.VMEM((NT, RANK, 128), BF16),
        pltpu.VMEM((4, 16, 128), BF16),
        pltpu.VMEM((NY, NX, NZ, 16, 128), BF16),
        dma((5, 2)),
    ]
    for shape in ((2, 8, NX), (3,), (4,), (2, 3), (2, 5), (2, 2), (2, 15), (2, 4), (3,), (7,), (8,), (2, 15), (2, 16)):
        scratch += [dma(shape), dma(shape)]
    scratch += [pltpu.SemaphoreType.REGULAR] * 2 + [dma((6,))]
    out_shape = (
        jax.ShapeDtypeStruct((ROWS, COLS), BF16),
        jax.ShapeDtypeStruct((RANK, ROWS), F32),
        jax.ShapeDtypeStruct((RANK, 1024), F32),
    )
    results = pl.pallas_call(
        kernel,
        out_shape=out_shape,
        in_specs=[hbm] * 3,
        out_specs=(hbm,) * 3,
        scratch_shapes=scratch,
        compiler_params=pltpu.CompilerParams(collective_id=0, has_side_effects=True, vmem_limit_bytes=60 << 20),
        name="powersgd",
    )(grads[0, 0], error[0, 0], init_q.T)
    new_error, p_t, q_t = pl.pallas_call(
        emit,
        out_shape=out_shape,
        in_specs=[hbm] * 3,
        out_specs=(hbm,) * 3,
        scratch_shapes=[pltpu.VMEM(o.shape, o.dtype) for o in out_shape] + [dma((2, 5))],
        compiler_params=pltpu.CompilerParams(vmem_limit_bytes=60 << 20),
        name="emit",
    )(*results)
    return new_error[None, None], p_t.T[None], q_t.T


def solution(mesh):
    in_specs = (P(None, "dp", "tensor", None), P(None, "dp", "tensor", None), P("tensor", None))
    out_specs = (P(None, "dp", "tensor", None), P(None, "tensor", None), P("tensor", None))
    return jax.shard_map(body, mesh=mesh, in_specs=in_specs, out_specs=out_specs, check_vma=False)
```

```python
import jax
import jax.numpy as jnp
from jax import lax
from jax.experimental import pallas as pl
from jax.experimental.pallas import tpu as pltpu
from jax.sharding import PartitionSpec as P

F32 = jnp.float32
BF16 = jnp.bfloat16
MESH = pl.DeviceIdType.MESH
HIGH = lax.Precision.HIGHEST
NZ, NX, NY, NT = 16, 4, 4, 8
ROWS, COLS, RANK = 96, 8192, 64
SHIFT = 0.05
REPLICAS = 64
NT_DIMS = (((1,), (1,)), ((), ()))


def inverse_factor(gram_wide):
    n, k = RANK, 8
    lane = lax.broadcasted_iota(jnp.int32, (n, 2 * n), 1)
    row = lax.broadcasted_iota(jnp.int32, (n, 2 * n), 0)
    a = gram_wide + jnp.where(lane == row, SHIFT, 0.0) + jnp.where(lane == row + n, 1.0, 0.0)
    for first in range(0, n, k):
        cols = [jnp.broadcast_to(a[:, first + i : first + i + 1], (n, 2 * n)) for i in range(k)]
        rows = [jnp.broadcast_to(a[first + i : first + i + 1, :], (n, 2 * n)) for i in range(k)]
        for i in range(k):
            j = first + i
            f = jnp.where(row > j, cols[i] * (1.0 / cols[i][j : j + 1, :]), 0.0)
            for m in range(i + 1, k):
                cols[m] = cols[m] - f * cols[m][j : j + 1, :]
                rows[m] = rows[m] - f[first + m : first + m + 1, :] * rows[i]
            a = a - f * rows[i]
    pivot = jnp.sum(jnp.where(lane == row, a, 0.0), axis=1, keepdims=True)
    return jnp.where(lane >= n, a, 0.0) * lax.rsqrt(pivot)


def kernel(
    g_hbm, e_hbm, q_hbm, out_hbm, pf_hbm, qf_hbm,
    out, pf, qf, gv, ev, m2, mz, q0, rr, sz, xrb, mb, part, x_in, px, z1_in, pz, z2_in, pall, phf, phl, q2own, qbuf,
    ld, ring_s, ring_r, q0_s, q0_r, qs_s, qs_r, x_s, x_r, z1_s, z1_r, z2_s, z2_r, pa_s, pa_r, ps_s, ps_r,
    sx_s, sx_r, st_s, st_r, qz_s, qz_r, xy_s, xy_r, sb_s, sb_r, near, far, st_out,
):
    dp = lax.axis_index("dp")
    t = lax.axis_index("tensor")
    z, x = dp // NX, dp % NX
    y, c = t // 2, t % 2

    def dev(zz, xx, tt):
        return {"dp": zz * NX + xx, "tensor": tt}

    def rcopy(src, dst, s, r, device):
        return pltpu.make_async_remote_copy(src, dst, s, r, device_id=device, device_id_type=MESH)

    sent = []

    def send(make, *args, order):
        for o in order:
            make(*args, o).start()
        sent.append(lambda: [make(*args, o).wait_send() for o in order])

    barrier = pltpu.get_barrier_semaphore()

    def greet(device):
        pl.semaphore_signal(barrier, inc=1, device_id=device, device_id_type=MESH)

    def greet_xy(o, _):
        greet(dev(z, (x + o // NY) % NX, ((y + o % NY) % NY) * 2 + c))
        return 0

    def greet_t(o, _):
        greet(dev(z, x, ((y + o) % NY) * 2 + 1 - c))
        return 0

    for o in (2, NZ - 2, 1, NZ - 1):
        greet(dev((z + o) % NZ, x, t))
    lax.fori_loop(1, NX * NY, greet_xy, 0)
    lax.fori_loop(0, NY, greet_t, 0)

    def greet_far(step, sem):
        for o in (step, NZ - step):
            pl.semaphore_signal(sem, inc=1, device_id=dev((z + o) % NZ, x, t), device_id_type=MESH)

    def load(k, which):
        span = pl.ds(k * 2048, 2048)
        src, dst = ((g_hbm, gv), (e_hbm, ev))[which]
        return pltpu.make_async_copy(src.at[:, span], dst.at[:, span], ld.at[k, which])

    q_load = pltpu.make_async_copy(q_hbm, q0.at[t], ld.at[4, 0])
    q_load.start()
    for k in range(4):
        load(k, 0).start()
        load(k, 1).start()
    mb[:, pl.ds(ROWS, 32), :] = jnp.zeros((NT, 32, 128), BF16)
    part[...] = jnp.zeros((2, 4, 16, 128), F32)
    for k in range(4):
        load(k, 0).wait()
        load(k, 1).wait()

        def add_block(j, _, k=k):
            at = pl.ds(pl.multiple_of(k * 2048 + j * 128, 128), 128)
            block = (gv[:, at].astype(F32) + ev[:, at].astype(F32)).astype(BF16)
            m2[:, at] = block
            mz[k * 16 + j] = block
            return 0

        lax.fori_loop(0, 16, add_block, 0)
    q_load.wait()
    pl.semaphore_wait(barrier, 23)

    def ring(d, s, xb):
        device = dev((z + (1 if d == 0 else NZ - 1)) % NZ, x, t)
        sems = (ring_s.at[d, s - 1, xb], ring_r.at[d, s - 1, xb])
        if s == 1:
            half = pl.ds(48 * d, 48)
            at = ((z + 8) % NZ) * NX + xb
            return rcopy(mz.at[at, half], rr.at[d, 0, xb, half], *sems, device)
        return rcopy(rr.at[d, s - 2, xb], rr.at[d, s - 1, xb], *sems, device)

    def ring_step(s):
        def one(xb, _):
            for d in range(2):
                if s > 1:
                    ring(d, s - 1, xb).wait_recv()
                    hops = 9 - s
                    at = ((z + (hops if d == 0 else NZ - hops)) % NZ) * NX + xb
                    if s == 2:
                        half, rest = pl.ds(48 * d, 48), pl.ds(48 - 48 * d, 48)
                        total = rr[d, 0, xb, half].astype(F32) + mz[at, half].astype(F32)
                        rr[d, 0, xb, half] = total.astype(BF16)
                        rr[d, 0, xb, rest] = mz[at, rest]
                    else:
                        total = rr[d, s - 2, xb].astype(F32) + mz[at].astype(F32)
                        rr[d, s - 2, xb] = total.astype(BF16)
                ring(d, s, xb).start()
            return 0

        lax.fori_loop(0, NX, one, 0)

        def ring_sent(xb, _):
            ring(0, s, xb).wait_send()
            ring(1, s, xb).wait_send()
            return 0

        sent.append(lambda: lax.fori_loop(0, NX, ring_sent, 0))

    def q0_copy(o):
        return rcopy(q0.at[t], q0.at[t], q0_s.at[o - 1], q0_r.at[o - 1], dev(z, x, ((y + o) % NY) * 2 + c))

    def q0_arrived(o):
        slot = q0.at[((y + NY - o) % NY) * 2 + c]
        return rcopy(slot, slot, q0_s.at[o - 1], q0_r.at[o - 1], dev(z, x, ((y + o) % NY) * 2 + c))

    def q0_pass(core, o):
        slot = q0.at[((y + NY - o) % NY) * 2 + core]
        return rcopy(slot, slot, qs_s.at[o], qs_r.at[o], dev(z, x, y * 2 + 1 - c))

    def xcopy(it, o):
        to = (x + o) % NX
        return rcopy(part.at[it, to], x_in.at[it, o - 1], x_s.at[it, o - 1], x_r.at[it, o - 1], dev(z, to, t))

    def z1copy(it, i):
        to = (z + (8, 2, 14, 1, 15)[i]) % NZ
        return rcopy(px.at[it], z1_in.at[it, i], z1_s.at[it, i], z1_r.at[it, i], dev(to, x, t))

    def z2copy(it, i):
        to = (z + (5, 11)[i]) % NZ
        return rcopy(pz.at[it], z2_in.at[it, i], z2_s.at[it, i], z2_r.at[it, i], dev(to, x, t))

    def pacopy(it, o, back=0):
        xo, yo = o // NY, o % NY
        slot = pall.at[it, c, (x + (NX - xo) * back) % NX, (y + (NY - yo) * back) % NY]
        to = dev(z, (x + xo) % NX, ((y + yo) % NY) * 2 + c)
        return rcopy(slot, slot, pa_s.at[it, o - 1], pa_r.at[it, o - 1], to)

    def pscopy(it, core, xo):
        slot = pall.at[it, core, (x + NX - xo) % NX]
        return rcopy(slot, slot, ps_s.at[it, xo], ps_r.at[it, xo], dev(z, x, y * 2 + 1 - c))

    def start_x(it):
        send(xcopy, it, order=(2, 1, 3))

    def x_to_z1(it):
        total = part[it, x]
        for o in (1, 3, 2):
            xcopy(it, o).wait_recv()
            total = total + x_in[it, o - 1]
        px[it] = total
        send(z1copy, it, order=range(5))

    def z1_to_z2(it):
        total = px[it]
        for i in (3, 4, 1, 2):
            z1copy(it, i).wait_recv()
            total = total + z1_in[it, i]
        pz[it] = total
        send(z2copy, it, order=range(2))

    def z2_to_plane(it):
        total = pz[it]
        z1copy(it, 0).wait_recv()
        total = total + z1_in[it, 0]
        for i in range(2):
            z2copy(it, i).wait_recv()
            total = total + z2_in[it, i]
        pall[it, c, x, y] = total * (1.0 / REPLICAS)

        def start(o, _):
            pacopy(it, o).start()
            return 0

        def leave(o, _):
            pacopy(it, o).wait_send()
            return 0

        lax.fori_loop(1, NX * NY, start, 0)
        sent.append(lambda: lax.fori_loop(1, NX * NY, leave, 0))

    def plane_to_sibling(it):
        def arrive(o, _):
            pacopy(it, o, 1).wait_recv()
            return 0

        for xo in (0, 1, 3, 2):
            lax.fori_loop(max(4 * xo, 1), 4 * xo + 4, arrive, 0)
            send(pscopy, it, c, order=(xo,))

    def finish_p(it):
        for xo in (0, 1, 3, 2):
            pscopy(it, 1 - c, xo).wait_recv()
        gram = jnp.zeros((RANK, 128), F32)
        zeros = jnp.zeros((RANK, 128), F32)
        for k in range(NT):
            block = pall[it, k % 2, :, k // 2].reshape(RANK, 128)
            wide = jnp.concatenate([block, zeros], axis=0)
            gram = gram + lax.dot_general(block, wide, NT_DIMS, precision=HIGH, preferred_element_type=F32)
        linv = inverse_factor(gram)
        for k in range(NT):
            block = jnp.concatenate([zeros, pall[it, k % 2, :, k // 2].reshape(RANK, 128)], axis=0)
            phat = jnp.dot(linv, block, precision=HIGH, preferred_element_type=F32)
            phf[k] = phat
            phl[k] = phat.astype(BF16)

    def next_q():
        total = jnp.zeros((RANK, 128), F32)
        for k in range(NT):
            total = total + jnp.dot(phl[k], mb[k], preferred_element_type=F32)
        return (total * (1.0 / REPLICAS)).astype(BF16)

    def sxcopy(o):
        to = (x + o) % NX
        return rcopy(sz.at[to], xrb.at[o - 1], sx_s.at[o - 1], sx_r.at[o - 1], dev(z, to, t))

    def stcopy(o, back=0):
        slot = mb.at[(t + (NT - o) * back) % NT, pl.ds(0, ROWS)]
        return rcopy(slot, slot, st_s.at[o - 1], st_r.at[o - 1], dev(z, x, (t + o) % NT))

    ring_step(1)
    greet_far(2, near)
    send(q0_copy, order=(2, 1, 3))
    send(q0_pass, c, order=(0,))
    pl.semaphore_wait(near, 2)
    greet_far(4, far)
    ring_step(2)
    ring_step(3)
    for o in (1, 3, 2):
        q0_arrived(o).wait_recv()
        send(q0_pass, c, order=(o,))
    def p_terms(core):
        total = jnp.zeros((RANK, ROWS), F32)
        for k in range(NY):
            at = 2 * k + core
            span = pl.ds(pl.multiple_of(at * 1024, 1024), 1024)
            total = total + lax.dot_general(q0[at], m2[:, span], NT_DIMS, preferred_element_type=F32)
        return total

    part[0, :, :, 0:ROWS] = p_terms(c).reshape(4, 16, ROWS)
    ring_step(4)
    pl.semaphore_wait(far, 2)
    for o in range(NY):
        q0_pass(1 - c, o).wait_recv()
    first_p = part[0, :, :, 0:ROWS].reshape(RANK, ROWS) + p_terms(1 - c)
    part[0, :, :, 0:ROWS] = first_p.reshape(4, 16, ROWS)
    start_x(0)
    ring_step(5)
    x_to_z1(0)
    ring_step(6)
    z1_to_z2(0)
    ring_step(7)
    ring_step(8)
    z2_to_plane(0)

    def ring_end(xb, _):
        ring(0, 8, xb).wait_recv()
        ring(1, 8, xb).wait_recv()
        total = rr[0, 7, xb].astype(F32) + rr[1, 7, xb].astype(F32) + mz[z * NX + xb].astype(F32)
        sz[xb] = total.astype(BF16)

        @pl.when(xb != x)
        def _():
            sxcopy((xb + NX - x) % NX).start()

        return 0

    lax.fori_loop(0, NX, ring_end, 0)
    sent.append(lambda: [sxcopy(o).wait_send() for o in (1, 2, 3)])
    plane_to_sibling(0)
    total = sz[x].astype(F32)
    for o in (1, 3, 2):
        sxcopy(o).wait_recv()
        total = total + xrb[o - 1].astype(F32)
    mb[t, pl.ds(0, ROWS)] = total.astype(BF16)
    send(stcopy, order=range(1, NT))
    finish_p(0)
    for o in range(1, NT):
        stcopy(o, 1).wait_recv()
    q1 = next_q()
    second_p = lax.dot_general(q1, mb[t], NT_DIMS, preferred_element_type=F32)
    part[1] = second_p.reshape(4, 16, 128)
    start_x(1)
    x_to_z1(1)
    z1_to_z2(1)
    z2_to_plane(1)
    plane_to_sibling(1)
    finish_p(1)
    q2own[...] = next_q().reshape(4, 16, 128)

    def qz_slot(k):
        return (NZ - k) * (1 - c) + k * c

    def qz_copy(k):
        to = (z + k * (1 - c) + (NZ - k) * c) % NZ
        return rcopy(q2own.at[y], qbuf.at[y, x, qz_slot(k)], qz_s.at[k - 1], qz_r.at[k - 1], dev(to, x, t))

    @pl.when(c == 0)
    def _():
        qz_copy(8).start()

    def far_sent():
        @pl.when(c == 0)
        def _():
            qz_copy(8).wait_send()

    sent.append(far_sent)
    send(qz_copy, order=range(7, 0, -1))

    @pl.when(c == 1)
    def _():
        qbuf[y, x, 0] = q2own[y]

    own = phf[t]
    pf[...] = own[:, 0:ROWS]
    pf_copy = pltpu.make_async_copy(pf, pf_hbm, st_out.at[4])
    pf_copy.start()
    p_rows = jnp.transpose(own)[0:ROWS, :].astype(BF16)

    def plane_span(half, core):
        return pl.ds((12 - 4 * half) * (1 - core) + 4 * half * core, 4)

    def xy_copy(half, o, back=0):
        xo, yo = o // NY, o % NY
        slot = qbuf.at[(y + (NY - yo) * back) % NY, (x + (NX - xo) * back) % NX, plane_span(half, c)]
        to = dev(z, (x + xo) % NX, ((y + yo) % NY) * 2 + c)
        return rcopy(slot, slot, xy_s.at[half, o - 1], xy_r.at[half, o - 1], to)

    def sib_copy(half, o, core):
        xo, yo = o // NY, o % NY
        slot = qbuf.at[(y + NY - yo) % NY, (x + NX - xo) % NX, plane_span(half, core)]
        return rcopy(slot, slot, sb_s.at[half, o], sb_r.at[half, o], dev(z, x, y * 2 + 1 - c))

    def to_plane(half):
        def start(o, _):
            xy_copy(half, o).start()
            return 0

        def leave(o, _):
            xy_copy(half, o).wait_send()
            return 0

        def leave_sibling(o, _):
            sib_copy(half, o, c).wait_send()
            return 0

        lax.fori_loop(1, NX * NY, start, 0)
        sib_copy(half, 0, c).start()
        sent.append(lambda: lax.fori_loop(1, NX * NY, leave, 0))
        sent.append(lambda: lax.fori_loop(0, NX * NY, leave_sibling, 0))

    def from_plane(half, xo):
        def arrive(o, _):
            xy_copy(half, o, 1).wait_recv()
            sib_copy(half, o, c).start()
            return 0

        lax.fori_loop(max(4 * xo, 1), 4 * xo + 4, arrive, 0)

    def compute(half, xo):
        def sib_wait(o, _):
            sib_copy(half, o, 1 - c).wait_recv()
            return 0

        lax.fori_loop(4 * xo, 4 * xo + 4, sib_wait, 0)
        xx = (x + NX - xo) % NX
        for first in (12 - 4 * half, 4 * half):
            for r in range(first, first + 4):
                at = pl.ds(pl.multiple_of((((z + r) % NZ) * NX + xx) * 128, 128), 128)
                approx = jnp.dot(p_rows, qbuf[:, xx, r].reshape(RANK, 128), preferred_element_type=F32)
                summed = gv[:, at].astype(F32) + ev[:, at].astype(F32)
                out[:, at] = (summed - approx).astype(BF16)
                pltpu.make_async_copy(out.at[:, at], out_hbm.at[:, at], st_out.at[xo]).start()

    for k in range(1, 4):
        qz_copy(k).wait_recv()

    @pl.when(c == 0)
    def _():
        qz_copy(4).wait_recv()

    to_plane(0)

    @pl.when(c == 1)
    def _():
        qz_copy(4).wait_recv()

    for k in range(5, 8):
        qz_copy(k).wait_recv()

    @pl.when(c == 0)
    def _():
        qz_copy(8).wait_recv()

    to_plane(1)
    for xo in range(NX):
        from_plane(0, xo)
    for xo in range(NX):
        compute(0, xo)
        from_plane(1, xo)
    for xo in range(NX):
        compute(1, xo)
    for i in range(8):
        r = (2 * t + i // NX + NZ - z) % NZ
        qf[:, i * 128 : (i + 1) * 128] = qbuf[:, i % NX, r].reshape(RANK, 128).astype(F32)

    qf_copy = pltpu.make_async_copy(qf, qf_hbm, st_out.at[5])
    qf_copy.start()
    for wait in sent:
        wait()
    pf_copy.wait()
    qf_copy.wait()
    for xo in range(NX):
        part_of = pl.ds(xo * 2048, 2048)
        pltpu.make_async_copy(out.at[:, part_of], out_hbm.at[:, part_of], st_out.at[xo]).wait()


def emit(a, b, d, out_a, out_b, out_d, va, vb, vd, sem):
    rows = [pl.ds(i * 32, 32) for i in range(3)]
    pieces = [(a.at[r], va.at[r], out_a.at[r]) for r in rows] + [(b, vb, out_b), (d, vd, out_d)]
    loads = [pltpu.make_async_copy(src, mid, sem.at[0, i]) for i, (src, mid, _) in enumerate(pieces)]
    stores = [pltpu.make_async_copy(mid, dst, sem.at[1, i]) for i, (_, mid, dst) in enumerate(pieces)]
    for load in loads:
        load.start()
    for load, store in zip(loads, stores):
        load.wait()
        store.start()
    for store in stores:
        store.wait()


def body(grads, error, init_q):
    hbm = pl.BlockSpec(memory_space=pltpu.HBM)
    dma = pltpu.SemaphoreType.DMA
    scratch = [
        pltpu.VMEM((ROWS, COLS), BF16),
        pltpu.VMEM((RANK, ROWS), F32),
        pltpu.VMEM((RANK, 1024), F32),
        pltpu.VMEM((ROWS, COLS), BF16),
        pltpu.VMEM((ROWS, COLS), BF16),
        pltpu.VMEM((ROWS, COLS), BF16),
        pltpu.VMEM((64, ROWS, 128), BF16),
        pltpu.VMEM((NT, RANK, 1024), BF16),
        pltpu.VMEM((2, 8, NX, ROWS, 128), BF16),
        pltpu.VMEM((NX, ROWS, 128), BF16),
        pltpu.VMEM((3, ROWS, 128), BF16),
        pltpu.VMEM((NT, 128, 128), BF16),
        pltpu.VMEM((2, 4, 16, 128), F32),
        pltpu.VMEM((2, 3, 16, 128), F32),
        pltpu.VMEM((2, 16, 128), F32),
        pltpu.VMEM((2, 5, 16, 128), F32),
        pltpu.VMEM((2, 16, 128), F32),
        pltpu.VMEM((2, 2, 16, 128), F32),
        pltpu.VMEM((2, 2, NX, NY, 16, 128), F32),
        pltpu.VMEM((NT, RANK, 128), F32),
        pltpu.VMEM((NT, RANK, 128), BF16),
        pltpu.VMEM((4, 16, 128), BF16),
        pltpu.VMEM((NY, NX, NZ, 16, 128), BF16),
        dma((5, 2)),
    ]
    for shape in ((2, 8, NX), (3,), (4,), (2, 3), (2, 5), (2, 2), (2, 15), (2, 4), (3,), (7,), (8,), (2, 15), (2, 16)):
        scratch += [dma(shape), dma(shape)]
    scratch += [pltpu.SemaphoreType.REGULAR] * 2 + [dma((6,))]
    out_shape = (
        jax.ShapeDtypeStruct((ROWS, COLS), BF16),
        jax.ShapeDtypeStruct((RANK, ROWS), F32),
        jax.ShapeDtypeStruct((RANK, 1024), F32),
    )
    results = pl.pallas_call(
        kernel,
        out_shape=out_shape,
        in_specs=[hbm] * 3,
        out_specs=(hbm,) * 3,
        scratch_shapes=scratch,
        compiler_params=pltpu.CompilerParams(collective_id=0, has_side_effects=True, vmem_limit_bytes=60 << 20),
        name="powersgd",
    )(grads[0, 0], error[0, 0], init_q.T)
    new_error, p_t, q_t = pl.pallas_call(
        emit,
        out_shape=out_shape,
        in_specs=[hbm] * 3,
        out_specs=(hbm,) * 3,
        scratch_shapes=[pltpu.VMEM(o.shape, o.dtype) for o in out_shape] + [dma((2, 5))],
        compiler_params=pltpu.CompilerParams(vmem_limit_bytes=60 << 20),
        name="emit",
    )(*results)
    return new_error[None, None], p_t.T[None], q_t.T


def solution(mesh):
    in_specs = (P(None, "dp", "tensor", None), P(None, "dp", "tensor", None), P("tensor", None))
    out_specs = (P(None, "dp", "tensor", None), P(None, "tensor", None), P("tensor", None))
    return jax.shard_map(body, mesh=mesh, in_specs=in_specs, out_specs=out_specs, check_vma=False)
```
